128 devices in a mesh: tm: 32 (over y, x, core), cluster: 4 (over z).
Axes of the slice: x: 4, y: 4, z: 4, core: 2. Of those that a mesh axis runs over, the one named last changes fastest.
Arguments:
- cotangent: bfloat16 [32, 12288, 512], P(None, ('cluster', 'tm')), may hold values from -6 to 6
- propagated: bfloat16 [32, 12288, 512], P('tm', 'cluster'), may hold values from -0.0546875 to 0.0546875
- weight: bfloat16 [32, 512, 512], P('tm'), may hold values from -0.25 to 0.25
- block_rows: int32 [32, 4, 128], P('tm', 'cluster'), may hold values from 0 to 23
- block_cols: int32 [32, 4, 128], P('tm', 'cluster'), may hold values from 0 to 23
- block_values: bfloat16 [32, 4, 128, 128, 128], P('tm', 'cluster'), may hold values from -0.21875 to 0.21875
- block_counts: int32 [32, 4], P('tm', 'cluster'), may hold values from 1 to 128, as said below
- band: int32 [32], replicated, may hold values from 1 to 4, as said below
Outputs:
- input_grad: bfloat16 [32, 12288, 512], P(None, ('cluster', 'tm'))
- weight_grad: float32 [32, 512, 512], P('tm')
The draws below stay inside these ranges and needn't reach their ends.
Inputs may be any that keep to these rules, and one draw needn't show every extreme that they name: `block_counts`: slots past the count are ignored; the last snapshot has 128 live blocks in some cluster. Some snapshot has band width 4.
All inputs are finite; a program needn't handle non-finite values.
Results may differ from the reference program's by a relative error of at most 0.014.
Values may be sent and summed in bfloat16 or wider, within the bound.
No kernel may reach another device: no remote copies, remote signals or barrier semaphores. Data moves between devices by JAX's collectives and lax.ppermute only.
A program may use at most 192 MiB of HBM per device.

```python
import jax
import jax.numpy as jnp
from jax import lax

F = 512
BLK = 128
VC = 3072
NB = 128
BAND = 4
SNAPS = 32
VERTS = 12288
N_CLUSTER = 4


def draw_block_counts(key, part):
    key = jax.random.fold_in(key, 11)
    first, second = jax.random.split(key, 2)
    lowest = max(NB // 4, 1)
    snap = jnp.arange(SNAPS, dtype=jnp.int32)[:, None]
    base = lowest + (NB - lowest) * snap // max(SNAPS - 1, 1)
    jitter = jax.random.randint(first, (SNAPS, N_CLUSTER), 0, lowest + 1)
    counts = jnp.clip(base - jitter, 1, NB)
    which = jax.random.randint(second, (), 0, N_CLUSTER)
    counts = counts.at[SNAPS - 1, which].set(NB)
    return counts.astype(jnp.int32)


def draw_band(key, part):
    key = jax.random.fold_in(key, 12)
    first, second = jax.random.split(key, 2)
    widths = jax.random.randint(first, (SNAPS,), 1, BAND + 1)
    where_full = jax.random.randint(second, (), 0, SNAPS)
    widths = widths.at[where_full].set(BAND)
    return widths.astype(jnp.int32)


def set_ends(values, rng, least, high):
    longest = values.shape.index(max(values.shape))
    spots = []
    for shift in (0, 1):
        where = [jax.random.randint(jax.random.fold_in(rng, axis), (), 0, length) for axis, length in enumerate(values.shape)]
        where[longest] = (where[longest] + shift) % values.shape[longest]
        spots.append(tuple(where))
    return values.at[spots[0]].set(least).at[spots[1]].set(high)


def level_of(stream_key, dims, cuts, low, top_value):
    gain = 1.0
    for position, shards_of in cuts:
        heights = jax.random.uniform(jax.random.fold_in(jax.random.fold_in(stream_key, 6), position), (shards_of,), jnp.float32, low / len(cuts), top_value / len(cuts))
        gain = gain * jnp.repeat(jnp.exp(heights), dims[position] // shards_of).reshape((-1,) + (1,) * (len(dims) - 1 - position))
    return gain


def scatter_about(own_key, extent, deviation, most, cuts=(), kind=jnp.bfloat16):
    array = jax.random.normal(own_key, extent, jnp.float32) * deviation
    if len(cuts) > 0:
        array = level_of(own_key, extent, cuts, -0.22, 0.18) * array
    return jnp.clip(array, min=-most, max=most).astype(kind)


def setup_inputs(seed: int = 0) -> dict:
    keys = jax.random.split(jax.random.key(seed), 9)
    return {
        "cotangent": scatter_about(keys[0], (SNAPS, VERTS, F), 1.0, 6.0, ((1, 128),)),
        "propagated": scatter_about(keys[1], (SNAPS, VERTS, F), VERTS ** -0.5, 0.0546875, ((0, 32), (1, 4))),
        "weight": scatter_about(keys[2], (SNAPS, F, F), F ** -0.5, 0.25, ((0, 32),)),
        "block_rows": set_ends(jax.random.randint(keys[3], (SNAPS, N_CLUSTER, NB), 0, VC // 128), jax.random.fold_in(keys[3], 1), 0, (VC // 128) - 1).astype(jnp.int32),
        "block_cols": set_ends(jax.random.randint(keys[4], (SNAPS, N_CLUSTER, NB), 0, VC // 128), jax.random.fold_in(keys[4], 1), 0, (VC // 128) - 1).astype(jnp.int32),
        "block_values": scatter_about(keys[5], (SNAPS, N_CLUSTER, NB, BLK, BLK), (NB * 128 // (VC // 128)) ** -0.5, 0.21875, ((0, 32), (1, 4))),
        "block_counts": draw_block_counts(jax.random.fold_in(keys[8], 71), 0),
        "band": draw_band(jax.random.fold_in(keys[8], 71), 0),
    }


def band_weights(band):
    total = band.shape[0]
    start = jnp.arange(total, dtype=jnp.int32)[:, None]
    offset = jnp.arange(BAND, dtype=jnp.int32)[None, :]
    target = start + offset
    widths = band[jnp.minimum(target, total - 1)]
    valid = (target < total) & (offset < widths)
    return jnp.where(valid, 1.0 / widths.astype(jnp.float32), 0.0).astype(jnp.float32)


def transpose_band(field, weights):
    total = field.shape[0]
    result = jnp.zeros(field.shape, jnp.float32)
    for offset in range(BAND):
        later = jnp.concatenate([field[offset:], jnp.zeros((offset,) + field.shape[1:], field.dtype)], axis=0)
        result = result + weights[:, offset][:, None, None] * later.astype(jnp.float32)
    return result


def transposed_hop(feats, rows, cols, values, count):
    nrows = feats.shape[0] // 128
    tiles = feats.reshape(nrows, 128, feats.shape[1])
    picked = tiles[rows]
    prod = jnp.einsum('bij,bif->bjf', values.astype(jnp.float32), picked.astype(jnp.float32))
    live = jnp.arange(rows.shape[0], dtype=jnp.int32) < count
    prod = jnp.where(live[:, None, None], prod, 0.0)
    result = jnp.zeros((nrows, 128, feats.shape[1]), jnp.float32).at[cols].add(prod)
    return result.reshape(feats.shape)


def reference(cotangent, propagated, weight, block_rows, block_cols, block_values, block_counts, band):
    weights = band_weights(band)
    dz = transpose_band(cotangent, weights).astype(jnp.bfloat16)
    clusters = block_rows.shape[1]

    def one_snapshot(snap):
        dz_t = dz[snap].reshape(clusters, -1, dz.shape[2])
        prop_t = propagated[snap].reshape(clusters, -1, dz.shape[2])
        wgrad = jnp.einsum('cvf,cvg->fg', prop_t.astype(jnp.float32), dz_t.astype(jnp.float32))
        pushed = jnp.einsum('cvg,fg->cvf', dz_t.astype(jnp.float32), weight[snap].astype(jnp.float32)).astype(jnp.bfloat16)
        hop = jax.vmap(transposed_hop)
        first = hop(pushed, block_rows[snap], block_cols[snap], block_values[snap], block_counts[snap]).astype(jnp.bfloat16)
        second = hop(first, block_rows[snap], block_cols[snap], block_values[snap], block_counts[snap]).astype(jnp.bfloat16)
        return second.reshape(-1, dz.shape[2]), wgrad

    second_hop, weight_grad = lax.map(one_snapshot, jnp.arange(band.shape[0], dtype=jnp.int32))
    input_grad = transpose_band(second_hop, weights).astype(jnp.bfloat16)
    return input_grad, weight_grad
```

```python
import functools

import jax
import jax.numpy as jnp
from jax import lax
from jax.experimental import pallas as pl
from jax.experimental.pallas import tpu as pltpu
from jax.sharding import PartitionSpec as P

BAND = 4
BLK = 128
UNROLL = 16
bf16 = jnp.bfloat16
f32 = jnp.float32
VMEM_LIMIT = 56 * 2**20


def band_kernel(band_ref, field_ref, out_ref):
    total = field_ref.shape[0]
    widths = [band_ref[t] for t in range(total)]
    scales = [
        jnp.where(
            width == 1,
            f32(1.0),
            jnp.where(width == 2, f32(0.5), jnp.where(width == 3, f32(1.0 / 3.0), f32(0.25))),
        )
        for width in widths
    ]
    window = [field_ref[t].astype(f32) for t in range(BAND)]
    for s in range(total):
        result = scales[s] * window[0]
        for offset in range(1, BAND):
            if s + offset < total:
                factor = jnp.where(offset < widths[s + offset], scales[s + offset], f32(0.0))
                result = result + factor * window[offset]
        out_ref[s] = result.astype(out_ref.dtype)
        window = window[1:]
        if s + BAND < total:
            window.append(field_ref[s + BAND].astype(f32))


def band_apply(band, field, rows=16):
    total, verts, width = field.shape
    spec = pl.BlockSpec((total, rows, width), lambda i: (0, i, 0))
    return pl.pallas_call(
        band_kernel,
        grid=(verts // rows,),
        in_specs=[pl.BlockSpec(memory_space=pltpu.SMEM), spec],
        out_specs=spec,
        out_shape=jax.ShapeDtypeStruct(field.shape, bf16),
        compiler_params=pltpu.CompilerParams(vmem_limit_bytes=VMEM_LIMIT),
    )(band, field)


def prepare_kernel(
    rows_ref, cols_ref, count_ref, values_ref, weight_ref,
    tiles_ref, slot_rows_ref, slot_cols_ref, slots_ref, weight_t_ref, sizes, used,
):
    col_tiles = sizes.shape[0]
    slot_total = slot_cols_ref.shape[0]
    count = count_ref[0]
    tiles_ref[...] = jnp.zeros_like(tiles_ref)
    weight_t_ref[...] = weight_ref[...].T

    def clear(s, carry):
        slot_cols_ref[s] = 0
        slot_rows_ref[2 * s] = 0
        slot_rows_ref[2 * s + 1] = 0
        return carry

    lax.fori_loop(0, slot_total, clear, 0)
    for c in range(col_tiles):
        sizes[c] = 0

    def tally(b, carry):
        c = cols_ref[b]
        sizes[c] = sizes[c] + 1
        return carry

    lax.fori_loop(0, count, tally, 0)
    first = jnp.int32(0)
    for c in range(col_tiles):
        used[c] = 2 * first
        first = first + (sizes[c] + 1) // 2
    slots_ref[0] = first

    def place(b, carry):
        c = cols_ref[b]
        half = used[c]
        used[c] = half + 1
        slot_rows_ref[half] = rows_ref[b]
        slot_cols_ref[half // 2] = c
        tiles_ref[half] = values_ref[b].T
        return carry

    lax.fori_loop(0, count, place, 0)


def prepare(rows, cols, count, values, weight, col_tiles):
    blocks = values.shape[0]
    slot_total = -(-(blocks // 2 + col_tiles // 2) // UNROLL) * UNROLL
    smem = pl.BlockSpec(memory_space=pltpu.SMEM)
    vmem = pl.BlockSpec(memory_space=pltpu.VMEM)
    return pl.pallas_call(
        prepare_kernel,
        in_specs=[smem, smem, smem, vmem, vmem],
        out_specs=(vmem, smem, smem, smem, vmem),
        out_shape=(
            jax.ShapeDtypeStruct((2 * slot_total, BLK, BLK), bf16),
            jax.ShapeDtypeStruct((2 * slot_total,), jnp.int32),
            jax.ShapeDtypeStruct((slot_total,), jnp.int32),
            jax.ShapeDtypeStruct((1,), jnp.int32),
            jax.ShapeDtypeStruct(weight.shape, bf16),
        ),
        scratch_shapes=[
            pltpu.SMEM((col_tiles,), jnp.int32),
            pltpu.SMEM((col_tiles,), jnp.int32),
        ],
        compiler_params=pltpu.CompilerParams(vmem_limit_bytes=VMEM_LIMIT),
    )(rows, cols, count, values, weight)


def hops_kernel(
    slot_rows_ref, slot_cols_ref, slots_ref, dz_ref, weight_t_ref, tiles_ref, out_ref, feats, acc
):
    tiles = feats.shape[0]
    group = 4
    for t in range(0, tiles, group):
        pushed = jnp.dot(
            dz_ref[t * BLK : (t + group) * BLK, :], weight_t_ref[...], preferred_element_type=f32
        ).astype(bf16)
        for k in range(group):
            feats[t + k] = pushed[k * BLK : (k + 1) * BLK]

    def step(q, carry):
        for u in range(UNROLL):
            slot = q * UNROLL + u
            left = jnp.concatenate([tiles_ref[2 * slot], tiles_ref[2 * slot + 1]], axis=1)
            right = jnp.concatenate(
                [feats[slot_rows_ref[2 * slot]], feats[slot_rows_ref[2 * slot + 1]]], axis=0
            )
            c = slot_cols_ref[slot]
            acc[c] = acc[c] + jnp.dot(left, right, preferred_element_type=f32)
        return carry

    trips = (slots_ref[0] + UNROLL - 1) // UNROLL
    acc[...] = jnp.zeros_like(acc)
    lax.fori_loop(0, trips, step, 0)
    feats[...] = acc[...].astype(bf16)
    acc[...] = jnp.zeros_like(acc)
    lax.fori_loop(0, trips, step, 0)
    for t in range(tiles):
        out_ref[t * BLK : (t + 1) * BLK, :] = acc[t].astype(bf16)


def two_hops(slot_rows, slot_cols, slots, dz, weight_t, tiles):
    verts, width = dz.shape
    smem = pl.BlockSpec(memory_space=pltpu.SMEM)
    vmem = pl.BlockSpec(memory_space=pltpu.VMEM)
    return pl.pallas_call(
        hops_kernel,
        in_specs=[smem, smem, smem, vmem, vmem, vmem],
        out_specs=vmem,
        out_shape=jax.ShapeDtypeStruct((verts, width), bf16),
        scratch_shapes=[
            pltpu.VMEM((verts // BLK, BLK, width), bf16),
            pltpu.VMEM((verts // BLK, BLK, width), f32),
        ],
        compiler_params=pltpu.CompilerParams(vmem_limit_bytes=VMEM_LIMIT),
    )(slot_rows, slot_cols, slots, dz, weight_t, tiles)


def exchange(field):
    return lax.all_to_all(field, "tm", split_axis=0, concat_axis=0, tiled=True)


def cluster_sum(terms, n):
    me = lax.axis_index("cluster")
    parts = terms.astype(bf16).reshape(n, terms.shape[0] // n, terms.shape[1])

    def shift(array, k):
        return lax.ppermute(array, "cluster", [(i, (i + k) % n) for i in range(n)])

    def pick(stack, k):
        return lax.dynamic_index_in_dim(stack, k % n, 0, keepdims=False)

    total = pick(parts, me).astype(f32)
    for k in range(1, n):
        total = total + shift(pick(parts, me + k), k).astype(f32)
    share = total.astype(bf16)
    shares = jnp.stack([share] + [shift(share, k) for k in range(1, n)])
    whole = jnp.concatenate([pick(shares, me + n - q) for q in range(n)], axis=0)
    return whole.astype(f32)


def on_device(
    n_cluster, cotangent, propagated, weight, block_rows, block_cols, block_values, block_counts, band
):
    snaps, own, width = cotangent.shape
    verts = snaps * own
    dz = exchange(band_apply(band, cotangent)).reshape(verts, width)
    tiles, slot_rows, slot_cols, slots, weight_t = prepare(
        block_rows[0, 0], block_cols[0, 0], block_counts[0], block_values[0, 0], weight[0], verts // BLK
    )
    second = two_hops(slot_rows, slot_cols, slots, dz, weight_t, tiles)
    input_grad = band_apply(band, exchange(second.reshape(snaps, own, width)))
    terms = jnp.einsum("vf,vg->fg", propagated[0], dz, preferred_element_type=f32)
    weight_grad = cluster_sum(terms, n_cluster)
    return (input_grad, weight_grad[None])


def solution(mesh):
    placed = (
        P(None, ("cluster", "tm"), None),
        P("tm", "cluster", None),
        P("tm", None, None),
        P("tm", "cluster", None),
        P("tm", "cluster", None),
        P("tm", "cluster", None, None, None),
        P("tm", "cluster"),
        P(),
    )
    return jax.shard_map(
        functools.partial(on_device, mesh.shape["cluster"]),
        mesh=mesh,
        in_specs=placed,
        out_specs=(P(None, ("cluster", "tm"), None), P("tm", None, None)),
        check_vma=False,
    )
```

```python
import functools

import jax
import jax.numpy as jnp
from jax import lax
from jax.experimental import pallas as pl
from jax.experimental.pallas import tpu as pltpu
from jax.sharding import PartitionSpec as P

BAND = 4
BLK = 128
UNROLL = 24
bf16 = jnp.bfloat16
f32 = jnp.float32
VMEM_LIMIT = 56 * 2**20


def band_kernel(group, band_ref, field_hbm, out_hbm, field, out, in_sems, out_sems):
    total, verts, width = field.shape
    groups = total // group
    rows, lanes = 16, 256

    def pull(g):
        part = pl.ds(g * group, group)
        return pltpu.make_async_copy(field_hbm.at[part], field.at[part], in_sems.at[g])

    def push(g):
        part = pl.ds(g * group, group)
        return pltpu.make_async_copy(out.at[part], out_hbm.at[part], out_sems.at[g])

    for g in range(groups):
        pull(g).start()
    widths = [band_ref[t] for t in range(total)]
    scales = [
        jnp.where(
            width == 1,
            f32(1.0),
            jnp.where(width == 2, f32(0.5), jnp.where(width == 3, f32(1.0 / 3.0), f32(0.25))),
        )
        for width in widths
    ]
    pull(0).wait()
    for g in range(groups):
        if g + 1 < groups:
            pull(g + 1).wait()
        start = g * group
        stop = min(start + group + BAND - 1, total)
        factors = [
            [scales[s]]
            + [
                jnp.where(o < widths[s + o], scales[s + o], f32(0.0))
                for o in range(1, BAND)
                if s + o < total
            ]
            for s in range(start, start + group)
        ]
        for row in range(0, verts, rows):
            for lane in range(0, width, lanes):
                spot = (pl.ds(row, rows), pl.ds(lane, lanes))
                window = [field[(t, *spot)].astype(f32) for t in range(start, stop)]
                for k in range(group):
                    result = factors[k][0] * window[k]
                    for o in range(1, len(factors[k])):
                        result = result + factors[k][o] * window[k + o]
                    out[(start + k, *spot)] = result.astype(out.dtype)
        push(g).start()
    for g in range(groups):
        push(g).wait()


def band_apply(band, field, group=4):
    total = field.shape[0]
    hbm = pl.BlockSpec(memory_space=pltpu.HBM)
    return pl.pallas_call(
        functools.partial(band_kernel, group),
        in_specs=[pl.BlockSpec(memory_space=pltpu.SMEM), hbm],
        out_specs=hbm,
        out_shape=jax.ShapeDtypeStruct(field.shape, bf16),
        scratch_shapes=[
            pltpu.VMEM(field.shape, bf16),
            pltpu.VMEM(field.shape, bf16),
            pltpu.SemaphoreType.DMA((total // group,)),
            pltpu.SemaphoreType.DMA((total // group,)),
        ],
        compiler_params=pltpu.CompilerParams(vmem_limit_bytes=VMEM_LIMIT),
    )(band, field)


def prepare_kernel(
    rows_ref, cols_ref, count_ref, values_ref, weight_ref,
    tiles_ref, slot_rows_ref, slot_cols_ref, slots_ref, weight_t_ref, sizes, used,
):
    col_tiles = sizes.shape[0]
    slot_total = slot_cols_ref.shape[0]
    count = count_ref[0]
    tiles_ref[...] = jnp.zeros_like(tiles_ref)
    weight_t_ref[...] = weight_ref[...].T

    def clear(s, carry):
        slot_cols_ref[s] = 0
        slot_rows_ref[2 * s] = 0
        slot_rows_ref[2 * s + 1] = 0
        return carry

    lax.fori_loop(0, slot_total, clear, 0)
    for c in range(col_tiles):
        sizes[c] = 0

    def tally(b, carry):
        c = cols_ref[b]
        sizes[c] = sizes[c] + 1
        return carry

    lax.fori_loop(0, count, tally, 0)
    first = jnp.int32(0)
    for c in range(col_tiles):
        used[c] = 2 * first
        first = first + (sizes[c] + 1) // 2
    slots_ref[0] = first

    def place(b, carry):
        c = cols_ref[b]
        half = used[c]
        used[c] = half + 1
        slot_rows_ref[half] = rows_ref[b]
        slot_cols_ref[half // 2] = c
        tiles_ref[half] = values_ref[b].T
        return carry

    lax.fori_loop(0, count, place, 0)


def prepare(rows, cols, count, values, weight, col_tiles):
    blocks = values.shape[0]
    slot_total = -(-(blocks // 2 + col_tiles // 2) // UNROLL) * UNROLL
    smem = pl.BlockSpec(memory_space=pltpu.SMEM)
    vmem = pl.BlockSpec(memory_space=pltpu.VMEM)
    return pl.pallas_call(
        prepare_kernel,
        in_specs=[smem, smem, smem, vmem, vmem],
        out_specs=(vmem, smem, smem, smem, vmem),
        out_shape=(
            jax.ShapeDtypeStruct((2 * slot_total, BLK, BLK), bf16),
            jax.ShapeDtypeStruct((2 * slot_total,), jnp.int32),
            jax.ShapeDtypeStruct((slot_total,), jnp.int32),
            jax.ShapeDtypeStruct((1,), jnp.int32),
            jax.ShapeDtypeStruct(weight.shape, bf16),
        ),
        scratch_shapes=[
            pltpu.SMEM((col_tiles,), jnp.int32),
            pltpu.SMEM((col_tiles,), jnp.int32),
        ],
        compiler_params=pltpu.CompilerParams(vmem_limit_bytes=VMEM_LIMIT),
    )(rows, cols, count, values, weight)


def hops_kernel(
    slot_rows_ref, slot_cols_ref, slots_ref, dz_hbm, weight_hbm, tiles_hbm, out_hbm,
    dz, weight_t, tiles_ref, feats, first, second, weight_sem, dz_sems, tile_sems, out_sems,
):
    tiles = feats.shape[0]
    group = tiles // dz_sems.shape[0]
    trips = (slots_ref[0] + UNROLL - 1) // UNROLL

    def pull(k):
        part = pl.ds(k * group * BLK, group * BLK)
        return pltpu.make_async_copy(dz_hbm.at[part], dz.at[part], dz_sems.at[k])

    def pull_tiles(q):
        part = pl.ds(q * 2 * UNROLL, 2 * UNROLL)
        return pltpu.make_async_copy(tiles_hbm.at[part], tiles_ref.at[part], tile_sems.at[q])

    def push(c):
        part = pl.ds(pl.multiple_of(c * BLK, BLK), BLK)
        return pltpu.make_async_copy(dz.at[part], out_hbm.at[part], out_sems.at[c])

    def start_tiles(q, carry):
        pull_tiles(q).start()
        return carry

    pull_weight = pltpu.make_async_copy(weight_hbm, weight_t, weight_sem)
    pull_weight.start()
    for k in range(tiles // group):
        pull(k).start()
    first[...] = jnp.zeros_like(first)
    second[...] = jnp.zeros_like(second)
    pull_weight.wait()
    for k in range(tiles // group):
        pull(k).wait()
        if k == tiles // group - 2:
            lax.fori_loop(0, trips, start_tiles, 0)
        pushed = jnp.dot(
            dz[k * group * BLK : (k + 1) * group * BLK, :], weight_t[...], preferred_element_type=f32
        ).astype(bf16)
        for t in range(group):
            feats[k * group + t] = pushed[t * BLK : (t + 1) * BLK]

    def work(q, acc):
        for u in range(UNROLL):
            slot = q * UNROLL + u
            left = jnp.concatenate([tiles_ref[2 * slot], tiles_ref[2 * slot + 1]], axis=1)
            right = jnp.concatenate(
                [feats[slot_rows_ref[2 * slot]], feats[slot_rows_ref[2 * slot + 1]]], axis=0
            )
            c = slot_cols_ref[slot]
            acc[c] = acc[c] + jnp.dot(left, right, preferred_element_type=f32)

    def first_hop(q, carry):
        pull_tiles(q).wait()
        work(q, first)
        return carry

    def second_hop(q, done):
        work(q, second)
        ahead = jnp.minimum((q + 1) * UNROLL, slot_cols_ref.shape[0] - 1)
        upto = jnp.where(q + 1 < trips, slot_cols_ref[ahead], tiles)

        def finish(c, carry):
            dz[pl.ds(pl.multiple_of(c * BLK, BLK), BLK), :] = second[c].astype(bf16)
            push(c).start()
            return carry

        lax.fori_loop(done, upto, finish, 0)
        return upto

    lax.fori_loop(0, trips, first_hop, 0)
    feats[...] = first[...].astype(bf16)
    lax.fori_loop(0, trips, second_hop, jnp.int32(0))
    for c in range(tiles):
        push(c).wait()


def two_hops(slot_rows, slot_cols, slots, dz, weight_t, tiles):
    verts, width = dz.shape
    col_tiles = verts // BLK
    parts = 4
    smem = pl.BlockSpec(memory_space=pltpu.SMEM)
    hbm = pl.BlockSpec(memory_space=pltpu.HBM)
    return pl.pallas_call(
        hops_kernel,
        in_specs=[smem, smem, smem, hbm, hbm, hbm],
        out_specs=hbm,
        out_shape=jax.ShapeDtypeStruct((verts, width), bf16),
        scratch_shapes=[
            pltpu.VMEM((verts, width), bf16),
            pltpu.VMEM(weight_t.shape, bf16),
            pltpu.VMEM(tiles.shape, bf16),
            pltpu.VMEM((col_tiles, BLK, width), bf16),
            pltpu.VMEM((col_tiles, BLK, width), f32),
            pltpu.VMEM((col_tiles, BLK, width), f32),
            pltpu.SemaphoreType.DMA,
            pltpu.SemaphoreType.DMA((parts,)),
            pltpu.SemaphoreType.DMA((tiles.shape[0] // (2 * UNROLL),)),
            pltpu.SemaphoreType.DMA((col_tiles,)),
        ],
        compiler_params=pltpu.CompilerParams(vmem_limit_bytes=VMEM_LIMIT),
    )(slot_rows, slot_cols, slots, dz, weight_t, tiles)


def exchange(field):
    return lax.all_to_all(field, "tm", split_axis=0, concat_axis=0, tiled=True)


def cluster_sum(terms, n):
    me = lax.axis_index("cluster")
    parts = terms.astype(bf16).reshape(n, terms.shape[0] // n, terms.shape[1])

    def shift(array, k):
        return lax.ppermute(array, "cluster", [(i, (i + k) % n) for i in range(n)])

    def pick(stack, k):
        return lax.dynamic_index_in_dim(stack, k % n, 0, keepdims=False)

    total = pick(parts, me).astype(f32)
    for k in range(1, n):
        total = total + shift(pick(parts, me + k), k).astype(f32)
    share = total.astype(bf16)
    shares = jnp.stack([share] + [shift(share, k) for k in range(1, n)])
    whole = jnp.concatenate([pick(shares, me + n - q) for q in range(n)], axis=0)
    return whole.astype(f32)


def on_device(
    n_cluster, cotangent, propagated, weight, block_rows, block_cols, block_values, block_counts, band
):
    snaps, own, width = cotangent.shape
    verts = snaps * own
    dz = exchange(band_apply(band, cotangent)).reshape(verts, width)
    tiles, slot_rows, slot_cols, slots, weight_t = prepare(
        block_rows[0, 0], block_cols[0, 0], block_counts[0], block_values[0, 0], weight[0], verts // BLK
    )
    second = two_hops(slot_rows, slot_cols, slots, dz, weight_t, tiles)
    input_grad = band_apply(band, exchange(second.reshape(snaps, own, width)))
    terms = jnp.einsum("vf,vg->fg", propagated[0], dz, preferred_element_type=f32)
    weight_grad = cluster_sum(terms, n_cluster)
    return (input_grad, weight_grad[None])


def solution(mesh):
    placed = (
        P(None, ("cluster", "tm"), None),
        P("tm", "cluster", None),
        P("tm", None, None),
        P("tm", "cluster", None),
        P("tm", "cluster", None),
        P("tm", "cluster", None, None, None),
        P("tm", "cluster"),
        P(),
    )
    return jax.shard_map(
        functools.partial(on_device, mesh.shape["cluster"]),
        mesh=mesh,
        in_specs=placed,
        out_specs=(P(None, ("cluster", "tm"), None), P("tm", None, None)),
        check_vma=False,
    )
```

```python
import functools

import jax
import jax.numpy as jnp
from jax import lax
from jax.experimental import pallas as pl
from jax.experimental.pallas import tpu as pltpu
from jax.sharding import PartitionSpec as P

BAND = 4
BLK = 128
SHORT = 8
LONG = 24
bf16 = jnp.bfloat16
f32 = jnp.float32
VMEM_LIMIT = 56 * 2**20


def band_kernel(group, band_ref, field_hbm, out_hbm, field, out, in_sems, out_sems):
    total, verts, width = field.shape
    groups = total // group
    rows, lanes = 16, 256

    def pull(g):
        part = pl.ds(g * group, group)
        return pltpu.make_async_copy(field_hbm.at[part], field.at[part], in_sems.at[g])

    def push(g):
        part = pl.ds(g * group, group)
        return pltpu.make_async_copy(out.at[part], out_hbm.at[part], out_sems.at[g])

    for g in range(groups):
        pull(g).start()
    widths = [band_ref[t] for t in range(total)]
    scales = [
        jnp.where(
            width == 1,
            f32(1.0),
            jnp.where(width == 2, f32(0.5), jnp.where(width == 3, f32(1.0 / 3.0), f32(0.25))),
        )
        for width in widths
    ]
    pull(0).wait()
    for g in range(groups):
        if g + 1 < groups:
            pull(g + 1).wait()
        start = g * group
        stop = min(start + group + BAND - 1, total)
        factors = [
            [scales[s]]
            + [
                jnp.where(o < widths[s + o], scales[s + o], f32(0.0))
                for o in range(1, BAND)
                if s + o < total
            ]
            for s in range(start, start + group)
        ]
        for row in range(0, verts, rows):
            for lane in range(0, width, lanes):
                spot = (pl.ds(row, rows), pl.ds(lane, lanes))
                window = [field[(t, *spot)].astype(f32) for t in range(start, stop)]
                for k in range(group):
                    result = factors[k][0] * window[k]
                    for o in range(1, len(factors[k])):
                        result = result + factors[k][o] * window[k + o]
                    out[(start + k, *spot)] = result.astype(out.dtype)
        push(g).start()
    for g in range(groups):
        push(g).wait()


def band_apply(band, field, group=4):
    total = field.shape[0]
    hbm = pl.BlockSpec(memory_space=pltpu.HBM)
    return pl.pallas_call(
        functools.partial(band_kernel, group),
        in_specs=[pl.BlockSpec(memory_space=pltpu.SMEM), hbm],
        out_specs=hbm,
        out_shape=jax.ShapeDtypeStruct(field.shape, bf16),
        scratch_shapes=[
            pltpu.VMEM(field.shape, bf16),
            pltpu.VMEM(field.shape, bf16),
            pltpu.SemaphoreType.DMA((total // group,)),
            pltpu.SemaphoreType.DMA((total // group,)),
        ],
        compiler_params=pltpu.CompilerParams(vmem_limit_bytes=VMEM_LIMIT),
    )(band, field)


def prepare_kernel(
    rows_ref, cols_ref, count_ref, values_ref, weight_ref,
    tiles_ref, slot_rows_ref, slot_cols_ref, slots_ref, weight_t_ref, sizes, used,
):
    col_tiles = sizes.shape[0]
    slot_total = slot_cols_ref.shape[0]
    count = count_ref[0]
    tiles_ref[...] = jnp.zeros_like(tiles_ref)
    weight_t_ref[...] = weight_ref[...].T

    def clear(s, carry):
        slot_cols_ref[s] = 0
        slot_rows_ref[2 * s] = 0
        slot_rows_ref[2 * s + 1] = 0
        return carry

    lax.fori_loop(0, slot_total, clear, 0)
    for c in range(col_tiles):
        sizes[c] = 0

    def tally(b, carry):
        c = cols_ref[b]
        sizes[c] = sizes[c] + 1
        return carry

    lax.fori_loop(0, count, tally, 0)
    first = jnp.int32(0)
    for c in range(col_tiles):
        used[c] = 2 * first
        first = first + (sizes[c] + 1) // 2
    slots_ref[0] = first

    def place(b, carry):
        c = cols_ref[b]
        half = used[c]
        used[c] = half + 1
        slot_rows_ref[half] = rows_ref[b]
        slot_cols_ref[half // 2] = c
        tiles_ref[half] = values_ref[b].T
        return carry

    lax.fori_loop(0, count, place, 0)


def prepare(rows, cols, count, values, weight, col_tiles):
    blocks = values.shape[0]
    slot_total = -(-(blocks // 2 + col_tiles // 2) // SHORT) * SHORT
    smem = pl.BlockSpec(memory_space=pltpu.SMEM)
    vmem = pl.BlockSpec(memory_space=pltpu.VMEM)
    return pl.pallas_call(
        prepare_kernel,
        in_specs=[smem, smem, smem, vmem, vmem],
        out_specs=(vmem, smem, smem, smem, vmem),
        out_shape=(
            jax.ShapeDtypeStruct((2 * slot_total, BLK, BLK), bf16),
            jax.ShapeDtypeStruct((2 * slot_total,), jnp.int32),
            jax.ShapeDtypeStruct((slot_total,), jnp.int32),
            jax.ShapeDtypeStruct((1,), jnp.int32),
            jax.ShapeDtypeStruct(weight.shape, bf16),
        ),
        scratch_shapes=[
            pltpu.SMEM((col_tiles,), jnp.int32),
            pltpu.SMEM((col_tiles,), jnp.int32),
        ],
        compiler_params=pltpu.CompilerParams(vmem_limit_bytes=VMEM_LIMIT),
    )(rows, cols, count, values, weight)


def hops_kernel(
    slot_rows_ref, slot_cols_ref, slots_ref, dz_hbm, weight_hbm, tiles_hbm, out_hbm,
    dz, weight_t, tiles_ref, feats, first, second, weight_sem, dz_sems, tile_sems, out_sems,
):
    tiles = feats.shape[0]
    group = tiles // dz_sems.shape[0]
    units = (slots_ref[0] + SHORT - 1) // SHORT
    trips = units // (LONG // SHORT)

    def pull(k):
        part = pl.ds(k * group * BLK, group * BLK)
        return pltpu.make_async_copy(dz_hbm.at[part], dz.at[part], dz_sems.at[k])

    def pull_tiles(q):
        part = pl.ds(q * 2 * SHORT, 2 * SHORT)
        return pltpu.make_async_copy(tiles_hbm.at[part], tiles_ref.at[part], tile_sems.at[q])

    def push(c):
        part = pl.ds(pl.multiple_of(c * BLK, BLK), BLK)
        return pltpu.make_async_copy(dz.at[part], out_hbm.at[part], out_sems.at[c])

    def start_tiles(q, carry):
        pull_tiles(q).start()
        return carry

    pull_weight = pltpu.make_async_copy(weight_hbm, weight_t, weight_sem)
    pull_weight.start()
    for k in range(tiles // group):
        pull(k).start()
    first[...] = jnp.zeros_like(first)
    second[...] = jnp.zeros_like(second)
    pull_weight.wait()
    for k in range(tiles // group):
        pull(k).wait()
        if k == 0:
            lax.fori_loop(0, units, start_tiles, 0)
        pushed = jnp.dot(
            dz[k * group * BLK : (k + 1) * group * BLK, :], weight_t[...], preferred_element_type=f32
        ).astype(bf16)
        for t in range(group):
            feats[k * group + t] = pushed[t * BLK : (t + 1) * BLK]

    def work(start, length, acc):
        for u in range(length):
            slot = start + u
            left = jnp.concatenate([tiles_ref[2 * slot], tiles_ref[2 * slot + 1]], axis=1)
            right = jnp.concatenate(
                [feats[slot_rows_ref[2 * slot]], feats[slot_rows_ref[2 * slot + 1]]], axis=0
            )
            c = slot_cols_ref[slot]
            acc[c] = acc[c] + jnp.dot(left, right, preferred_element_type=f32)

    def finish(c, carry):
        dz[pl.ds(pl.multiple_of(c * BLK, BLK), BLK), :] = second[c].astype(bf16)
        push(c).start()
        return carry

    def first_hop(length, q, carry):
        for k in range(length // SHORT):
            pull_tiles(q * (length // SHORT) + k).wait()
        work(q * length, length, first)
        return carry

    def second_hop(length, q, done):
        work(q * length, length, second)
        after = (q + 1) * length
        upto = jnp.where(
            after < units * SHORT,
            slot_cols_ref[jnp.minimum(after, slot_cols_ref.shape[0] - 1)],
            tiles,
        )
        lax.fori_loop(done, upto, finish, 0)
        return upto

    rest = trips * (LONG // SHORT)
    lax.fori_loop(0, trips, functools.partial(first_hop, LONG), 0)
    lax.fori_loop(rest, units, functools.partial(first_hop, SHORT), 0)
    feats[...] = first[...].astype(bf16)
    done = lax.fori_loop(0, trips, functools.partial(second_hop, LONG), jnp.int32(0))
    lax.fori_loop(rest, units, functools.partial(second_hop, SHORT), done)
    for c in range(tiles):
        push(c).wait()


def two_hops(slot_rows, slot_cols, slots, dz, weight_t, tiles):
    verts, width = dz.shape
    col_tiles = verts // BLK
    parts = 2
    smem = pl.BlockSpec(memory_space=pltpu.SMEM)
    hbm = pl.BlockSpec(memory_space=pltpu.HBM)
    return pl.pallas_call(
        hops_kernel,
        in_specs=[smem, smem, smem, hbm, hbm, hbm],
        out_specs=hbm,
        out_shape=jax.ShapeDtypeStruct((verts, width), bf16),
        scratch_shapes=[
            pltpu.VMEM((verts, width), bf16),
            pltpu.VMEM(weight_t.shape, bf16),
            pltpu.VMEM(tiles.shape, bf16),
            pltpu.VMEM((col_tiles, BLK, width), bf16),
            pltpu.VMEM((col_tiles, BLK, width), f32),
            pltpu.VMEM((col_tiles, BLK, width), f32),
            pltpu.SemaphoreType.DMA,
            pltpu.SemaphoreType.DMA((parts,)),
            pltpu.SemaphoreType.DMA((tiles.shape[0] // (2 * SHORT),)),
            pltpu.SemaphoreType.DMA((col_tiles,)),
        ],
        compiler_params=pltpu.CompilerParams(vmem_limit_bytes=VMEM_LIMIT),
    )(slot_rows, slot_cols, slots, dz, weight_t, tiles)


def exchange(field):
    return lax.all_to_all(field, "tm", split_axis=0, concat_axis=0, tiled=True)


def cluster_sum(terms, n):
    me = lax.axis_index("cluster")
    parts = terms.astype(bf16).reshape(n, terms.shape[0] // n, terms.shape[1])

    def shift(array, k):
        return lax.ppermute(array, "cluster", [(i, (i + k) % n) for i in range(n)])

    def pick(stack, k):
        return lax.dynamic_index_in_dim(stack, k % n, 0, keepdims=False)

    total = pick(parts, me).astype(f32)
    for k in range(1, n):
        total = total + shift(pick(parts, me + k), k).astype(f32)
    share = total.astype(bf16)
    shares = jnp.stack([share] + [shift(share, k) for k in range(1, n)])
    whole = jnp.concatenate([pick(shares, me + n - q) for q in range(n)], axis=0)
    return whole.astype(f32)


def on_device(
    n_cluster, cotangent, propagated, weight, block_rows, block_cols, block_values, block_counts, band
):
    snaps, own, width = cotangent.shape
    verts = snaps * own
    dz = exchange(band_apply(band, cotangent)).reshape(verts, width)
    tiles, slot_rows, slot_cols, slots, weight_t = prepare(
        block_rows[0, 0], block_cols[0, 0], block_counts[0], block_values[0, 0], weight[0], verts // BLK
    )
    second = two_hops(slot_rows, slot_cols, slots, dz, weight_t, tiles)
    input_grad = band_apply(band, exchange(second.reshape(snaps, own, width)))
    terms = jnp.einsum("vf,vg->fg", propagated[0], dz, preferred_element_type=f32)
    weight_grad = cluster_sum(terms, n_cluster)
    return (input_grad, weight_grad[None])


def solution(mesh):
    placed = (
        P(None, ("cluster", "tm"), None),
        P("tm", "cluster", None),
        P("tm", None, None),
        P("tm", "cluster", None),
        P("tm", "cluster", None),
        P("tm", "cluster", None, None, None),
        P("tm", "cluster"),
        P(),
    )
    return jax.shard_map(
        functools.partial(on_device, mesh.shape["cluster"]),
        mesh=mesh,
        in_specs=placed,
        out_specs=(P(None, ("cluster", "tm"), None), P("tm", None, None)),
        check_vma=False,
    )
```

```python
import functools

import jax
import jax.numpy as jnp
from jax import lax
from jax.experimental import pallas as pl
from jax.experimental.pallas import tpu as pltpu
from jax.sharding import PartitionSpec as P

BAND = 4
BLK = 128
SHORT = 8
LONG = 24
bf16 = jnp.bfloat16
f32 = jnp.float32
VMEM_LIMIT = 56 * 2**20


def band_kernel(group, band_ref, field, out_hbm, out, out_sems, pull=None):
    total, verts, width = field.shape
    groups = total // group
    rows, lanes = 16, 256

    def push(g):
        part = pl.ds(g * group, group)
        return pltpu.make_async_copy(out.at[part], out_hbm.at[part], out_sems.at[g])

    if pull is not None:
        for g in range(groups):
            pull(g).start()
    widths = [band_ref[t] for t in range(total)]
    scales = [
        jnp.where(
            width == 1,
            f32(1.0),
            jnp.where(width == 2, f32(0.5), jnp.where(width == 3, f32(1.0 / 3.0), f32(0.25))),
        )
        for width in widths
    ]
    if pull is not None:
        pull(0).wait()
    for g in range(groups):
        if pull is not None and g + 1 < groups:
            pull(g + 1).wait()
        start = g * group
        stop = min(start + group + BAND - 1, total)
        factors = [
            [scales[s]]
            + [
                jnp.where(o < widths[s + o], scales[s + o], f32(0.0))
                for o in range(1, BAND)
                if s + o < total
            ]
            for s in range(start, start + group)
        ]
        for row in range(0, verts, rows):
            for lane in range(0, width, lanes):
                spot = (pl.ds(row, rows), pl.ds(lane, lanes))
                window = [field[(t, *spot)].astype(f32) for t in range(start, stop)]
                for k in range(group):
                    result = factors[k][0] * window[k]
                    for o in range(1, len(factors[k])):
                        result = result + factors[k][o] * window[k + o]
                    out[(start + k, *spot)] = result.astype(out.dtype)
        push(g).start()
    for g in range(groups):
        push(g).wait()


def band_pull_kernel(group, band_ref, field_hbm, out_hbm, field, in_sems, out, out_sems):
    def pull(g):
        part = pl.ds(g * group, group)
        return pltpu.make_async_copy(field_hbm.at[part], field.at[part], in_sems.at[g])

    band_kernel(group, band_ref, field, out_hbm, out, out_sems, pull)


def band_apply(band, field, resident, group=4):
    total = field.shape[0]
    hbm = pl.BlockSpec(memory_space=pltpu.HBM)
    vmem = pl.BlockSpec(memory_space=pltpu.VMEM)
    staged = [pltpu.VMEM(field.shape, bf16), pltpu.SemaphoreType.DMA((total // group,))]
    return pl.pallas_call(
        functools.partial(band_kernel if resident else band_pull_kernel, group),
        in_specs=[pl.BlockSpec(memory_space=pltpu.SMEM), vmem if resident else hbm],
        out_specs=hbm,
        out_shape=jax.ShapeDtypeStruct(field.shape, bf16),
        scratch_shapes=staged * (1 if resident else 2),
        compiler_params=pltpu.CompilerParams(vmem_limit_bytes=(16 * 2**20 if resident else VMEM_LIMIT)),
    )(band, field)


def prepare_kernel(
    rows_ref, cols_ref, count_ref, values_hbm, weight_hbm,
    tiles_ref, slot_rows_ref, slot_cols_ref, slots_ref, weight_t_ref,
    values_ref, weight_ref, sizes, used, values_sem, weight_sem,
):
    col_tiles = sizes.shape[0]
    slot_total = slot_cols_ref.shape[0]
    count = count_ref[0]
    pull_weight = pltpu.make_async_copy(weight_hbm, weight_ref, weight_sem)
    pull_values = pltpu.make_async_copy(values_hbm, values_ref, values_sem)
    pull_weight.start()
    pull_values.start()
    tiles_ref[...] = jnp.zeros_like(tiles_ref)
    pull_weight.wait()
    weight_t_ref[...] = weight_ref[...].T

    def clear(s, carry):
        slot_cols_ref[s] = 0
        slot_rows_ref[2 * s] = 0
        slot_rows_ref[2 * s + 1] = 0
        return carry

    lax.fori_loop(0, slot_total, clear, 0)
    for c in range(col_tiles):
        sizes[c] = 0

    def tally(b, carry):
        c = cols_ref[b]
        sizes[c] = sizes[c] + 1
        return carry

    lax.fori_loop(0, count, tally, 0)
    first = jnp.int32(0)
    for c in range(col_tiles):
        used[c] = 2 * first
        first = first + (sizes[c] + 1) // 2
    slots_ref[0] = first

    def place(b, carry):
        c = cols_ref[b]
        half = used[c]
        used[c] = half + 1
        slot_rows_ref[half] = rows_ref[b]
        slot_cols_ref[half // 2] = c
        tiles_ref[half] = values_ref[b].T
        return carry

    pull_values.wait()
    lax.fori_loop(0, count, place, 0)


def prepare(rows, cols, count, values, weight, col_tiles):
    blocks = values.shape[0]
    slot_total = -(-(blocks // 2 + col_tiles // 2) // SHORT) * SHORT
    smem = pl.BlockSpec(memory_space=pltpu.SMEM)
    vmem = pl.BlockSpec(memory_space=pltpu.VMEM)
    hbm = pl.BlockSpec(memory_space=pltpu.HBM)
    return pl.pallas_call(
        prepare_kernel,
        in_specs=[smem, smem, smem, hbm, hbm],
        out_specs=(vmem, smem, smem, smem, vmem),
        out_shape=(
            jax.ShapeDtypeStruct((2 * slot_total, BLK, BLK), bf16),
            jax.ShapeDtypeStruct((2 * slot_total,), jnp.int32),
            jax.ShapeDtypeStruct((slot_total,), jnp.int32),
            jax.ShapeDtypeStruct((1,), jnp.int32),
            jax.ShapeDtypeStruct(weight.shape, bf16),
        ),
        scratch_shapes=[
            pltpu.VMEM(values.shape, bf16),
            pltpu.VMEM(weight.shape, bf16),
            pltpu.SMEM((col_tiles,), jnp.int32),
            pltpu.SMEM((col_tiles,), jnp.int32),
            pltpu.SemaphoreType.DMA,
            pltpu.SemaphoreType.DMA,
        ],
        compiler_params=pltpu.CompilerParams(vmem_limit_bytes=VMEM_LIMIT),
    )(rows, cols, count, values, weight)


def hops_kernel(
    slot_rows_ref, slot_cols_ref, slots_ref, dz, weight_hbm, tiles_hbm, out_hbm, dz_hbm,
    out, weight_t, tiles_ref, feats, first, second, weight_sem, tile_sems, out_sem, dz_sem,
):
    tiles = feats.shape[0]
    group = tiles // 2
    units = (slots_ref[0] + SHORT - 1) // SHORT
    trips = units // (LONG // SHORT)

    def pull_tiles(q):
        part = pl.ds(q * 2 * SHORT, 2 * SHORT)
        return pltpu.make_async_copy(tiles_hbm.at[part], tiles_ref.at[part], tile_sems.at[q])

    def push(c):
        part = pl.ds(pl.multiple_of(c * BLK, BLK), BLK)
        return pltpu.make_async_copy(out.at[part], out_hbm.at[part], out_sem)

    def start_tiles(q, carry):
        pull_tiles(q).start()
        return carry

    pull_weight = pltpu.make_async_copy(weight_hbm, weight_t, weight_sem)
    pull_weight.start()
    lax.fori_loop(0, units, start_tiles, 0)
    keep_dz = pltpu.make_async_copy(dz, dz_hbm, dz_sem)
    keep_dz.start()
    first[...] = jnp.zeros_like(first)
    second[...] = jnp.zeros_like(second)
    pull_weight.wait()
    for k in range(tiles // group):
        pushed = jnp.dot(
            dz[k * group * BLK : (k + 1) * group * BLK, :], weight_t[...], preferred_element_type=f32
        ).astype(bf16)
        for t in range(group):
            feats[k * group + t] = pushed[t * BLK : (t + 1) * BLK]

    def work(start, length, acc):
        for u in range(length):
            slot = start + u
            left = jnp.concatenate([tiles_ref[2 * slot], tiles_ref[2 * slot + 1]], axis=1)
            right = jnp.concatenate(
                [feats[slot_rows_ref[2 * slot]], feats[slot_rows_ref[2 * slot + 1]]], axis=0
            )
            c = slot_cols_ref[slot]
            acc[c] = acc[c] + jnp.dot(left, right, preferred_element_type=f32)

    def finish(c, carry):
        out[pl.ds(pl.multiple_of(c * BLK, BLK), BLK), :] = second[c].astype(bf16)
        push(c).start()
        return carry

    def first_hop(length, q, carry):
        for k in range(length // SHORT):
            pull_tiles(q * (length // SHORT) + k).wait()
        work(q * length, length, first)
        return carry

    def second_hop(length, q, done):
        work(q * length, length, second)
        after = (q + 1) * length
        upto = jnp.where(
            after < units * SHORT,
            slot_cols_ref[jnp.minimum(after, slot_cols_ref.shape[0] - 1)],
            tiles,
        )
        lax.fori_loop(done, upto, finish, 0)
        return upto

    rest = trips * (LONG // SHORT)
    lax.fori_loop(0, trips, functools.partial(first_hop, LONG), 0)
    lax.fori_loop(rest, units, functools.partial(first_hop, SHORT), 0)
    feats[...] = first[...].astype(bf16)
    done = lax.fori_loop(0, trips, functools.partial(second_hop, LONG), jnp.int32(0))
    lax.fori_loop(rest, units, functools.partial(second_hop, SHORT), done)
    keep_dz.wait()
    pltpu.make_async_copy(out, out_hbm, out_sem).wait()


def two_hops(slot_rows, slot_cols, slots, dz, weight_t, tiles):
    verts, width = dz.shape
    col_tiles = verts // BLK
    smem = pl.BlockSpec(memory_space=pltpu.SMEM)
    hbm = pl.BlockSpec(memory_space=pltpu.HBM)
    return pl.pallas_call(
        hops_kernel,
        in_specs=[smem, smem, smem, pl.BlockSpec(memory_space=pltpu.VMEM), hbm, hbm],
        out_specs=(hbm, hbm),
        out_shape=(pltpu.HBM((verts, width), bf16),) * 2,
        scratch_shapes=[
            pltpu.VMEM((verts, width), bf16),
            pltpu.VMEM(weight_t.shape, bf16),
            pltpu.VMEM(tiles.shape, bf16),
            pltpu.VMEM((col_tiles, BLK, width), bf16),
            pltpu.VMEM((col_tiles, BLK, width), f32),
            pltpu.VMEM((col_tiles, BLK, width), f32),
            pltpu.SemaphoreType.DMA,
            pltpu.SemaphoreType.DMA((tiles.shape[0] // (2 * SHORT),)),
            pltpu.SemaphoreType.DMA,
            pltpu.SemaphoreType.DMA,
        ],
        compiler_params=pltpu.CompilerParams(vmem_limit_bytes=48 * 2**20),
    )(slot_rows, slot_cols, slots, dz, weight_t, tiles)


def terms_kernel(left_hbm, right_hbm, out_ref, left, right, left_sem, right_sem):
    pull_left = pltpu.make_async_copy(left_hbm, left, left_sem)
    pull_right = pltpu.make_async_copy(right_hbm, right, right_sem)
    pull_left.start()
    pull_right.start()
    pull_left.wait()
    pull_right.wait()
    out_ref[...] = lax.dot_general(
        left[...], right[...], (((0,), (0,)), ((), ())), preferred_element_type=f32
    ).astype(bf16)


def gradient_terms(left, right):
    hbm = pl.BlockSpec(memory_space=pltpu.HBM)
    return pl.pallas_call(
        terms_kernel,
        in_specs=[hbm, hbm],
        out_specs=pl.BlockSpec(memory_space=pltpu.VMEM),
        out_shape=jax.ShapeDtypeStruct((left.shape[1], right.shape[1]), bf16),
        scratch_shapes=[
            pltpu.VMEM(left.shape, bf16),
            pltpu.VMEM(right.shape, bf16),
            pltpu.SemaphoreType.DMA,
            pltpu.SemaphoreType.DMA,
        ],
        compiler_params=pltpu.CompilerParams(vmem_limit_bytes=VMEM_LIMIT),
    )(left, right)


def exchange(field):
    return lax.all_to_all(field, "tm", split_axis=0, concat_axis=0, tiled=True)


def cluster_sum(terms, n):
    me = lax.axis_index("cluster")
    parts = terms.reshape(n, terms.shape[0] // n, terms.shape[1])

    def shift(array, k):
        return lax.ppermute(array, "cluster", [(i, (i + k) % n) for i in range(n)])

    def pick(stack, k):
        return lax.dynamic_index_in_dim(stack, k % n, 0, keepdims=False)

    total = pick(parts, me).astype(f32)
    for k in range(1, n):
        total = total + shift(pick(parts, me + k), k).astype(f32)
    share = total.astype(bf16)
    shares = jnp.stack([share] + [shift(share, k) for k in range(1, n)])
    whole = jnp.concatenate([pick(shares, me + n - q) for q in range(n)], axis=0)
    return whole.astype(f32)


def on_device(
    n_cluster, cotangent, propagated, weight, block_rows, block_cols, block_values, block_counts, band
):
    snaps, own, width = cotangent.shape
    verts = snaps * own
    dz = exchange(band_apply(band, cotangent, False)).reshape(verts, width)
    tiles, slot_rows, slot_cols, slots, weight_t = prepare(
        block_rows[0, 0], block_cols[0, 0], block_counts[0], block_values[0, 0], weight[0], verts // BLK
    )
    second, dz = two_hops(slot_rows, slot_cols, slots, dz, weight_t, tiles)
    input_grad = band_apply(band, exchange(second.reshape(snaps, own, width)), True)
    terms = gradient_terms(propagated[0], dz)
    weight_grad = cluster_sum(terms, n_cluster)
    return (input_grad, weight_grad[None])


def solution(mesh):
    placed = (
        P(None, ("cluster", "tm"), None),
        P("tm", "cluster", None),
        P("tm", None, None),
        P("tm", "cluster", None),
        P("tm", "cluster", None),
        P("tm", "cluster", None, None, None),
        P("tm", "cluster"),
        P(),
    )
    return jax.shard_map(
        functools.partial(on_device, mesh.shape["cluster"]),
        mesh=mesh,
        in_specs=placed,
        out_specs=(P(None, ("cluster", "tm"), None), P("tm", None, None)),
        check_vma=False,
    )
```

```python
import functools

import jax
import jax.numpy as jnp
from jax import lax
from jax.experimental import pallas as pl
from jax.experimental.pallas import tpu as pltpu
from jax.sharding import PartitionSpec as P

BAND = 4
BLK = 128
SHORT = 8
LONG = 24
bf16 = jnp.bfloat16
f32 = jnp.float32
VMEM_LIMIT = 56 * 2**20


def band_kernel(group, band_ref, field, out_hbm, out, out_sems, pull=None):
    total, verts, width = field.shape
    groups = total // group
    rows, lanes = 16, 256

    def push(g):
        part = pl.ds(g * group, group)
        return pltpu.make_async_copy(out.at[part], out_hbm.at[part], out_sems.at[g])

    if pull is not None:
        for g in range(groups):
            pull(g).start()
    widths = [band_ref[t] for t in range(total)]
    scales = [
        jnp.where(
            width == 1,
            f32(1.0),
            jnp.where(width == 2, f32(0.5), jnp.where(width == 3, f32(1.0 / 3.0), f32(0.25))),
        )
        for width in widths
    ]
    if pull is not None:
        pull(0).wait()
    for g in range(groups):
        if pull is not None and g + 1 < groups:
            pull(g + 1).wait()
        start = g * group
        stop = min(start + group + BAND - 1, total)
        factors = [
            [scales[s]]
            + [
                jnp.where(o < widths[s + o], scales[s + o], f32(0.0))
                for o in range(1, BAND)
                if s + o < total
            ]
            for s in range(start, start + group)
        ]
        for row in range(0, verts, rows):
            for lane in range(0, width, lanes):
                spot = (pl.ds(row, rows), pl.ds(lane, lanes))
                window = [field[(t, *spot)].astype(f32) for t in range(start, stop)]
                for k in range(group):
                    result = factors[k][0] * window[k]
                    for o in range(1, len(factors[k])):
                        result = result + factors[k][o] * window[k + o]
                    out[(start + k, *spot)] = result.astype(out.dtype)
        push(g).start()
    for g in range(groups):
        push(g).wait()


def band_pull_kernel(group, band_ref, field_hbm, out_hbm, field, in_sems, out, out_sems):
    def pull(g):
        part = pl.ds(g * group, group)
        return pltpu.make_async_copy(field_hbm.at[part], field.at[part], in_sems.at[g])

    band_kernel(group, band_ref, field, out_hbm, out, out_sems, pull)


def band_apply(band, field, resident, group=4):
    total = field.shape[0]
    hbm = pl.BlockSpec(memory_space=pltpu.HBM)
    vmem = pl.BlockSpec(memory_space=pltpu.VMEM)
    staged = [pltpu.VMEM(field.shape, bf16), pltpu.SemaphoreType.DMA((total // group,))]
    return pl.pallas_call(
        functools.partial(band_kernel if resident else band_pull_kernel, group),
        in_specs=[pl.BlockSpec(memory_space=pltpu.SMEM), vmem if resident else hbm],
        out_specs=hbm,
        out_shape=jax.ShapeDtypeStruct(field.shape, bf16),
        scratch_shapes=staged * (1 if resident else 2),
        compiler_params=pltpu.CompilerParams(vmem_limit_bytes=(16 * 2**20 if resident else VMEM_LIMIT)),
    )(band, field)


def split_table(table_ref, slot_total):
    return (
        table_ref.at[pl.ds(0, 2 * slot_total)],
        table_ref.at[pl.ds(2 * slot_total, slot_total)],
        table_ref.at[pl.ds(3 * slot_total, 1)],
    )


def prepare_kernel(
    rows_ref, cols_ref, count_ref, values_hbm, weight_hbm,
    tiles_ref, table_ref, weight_t_ref,
    values_ref, weight_ref, sizes, used, values_sem, weight_sem,
):
    col_tiles = sizes.shape[0]
    slot_total = tiles_ref.shape[0] // 2
    slot_rows_ref, slot_cols_ref, slots_ref = split_table(table_ref, slot_total)
    count = count_ref[0]
    pull_weight = pltpu.make_async_copy(weight_hbm, weight_ref, weight_sem)
    pull_values = pltpu.make_async_copy(values_hbm, values_ref, values_sem)
    pull_weight.start()
    pull_values.start()
    tiles_ref[...] = jnp.zeros_like(tiles_ref)
    pull_weight.wait()
    weight_t_ref[...] = weight_ref[...].T

    def clear(s, carry):
        slot_cols_ref[s] = 0
        slot_rows_ref[2 * s] = 0
        slot_rows_ref[2 * s + 1] = 0
        return carry

    lax.fori_loop(0, slot_total, clear, 0)
    for c in range(col_tiles):
        sizes[c] = 0

    def tally(b, carry):
        c = cols_ref[b]
        sizes[c] = sizes[c] + 1
        return carry

    lax.fori_loop(0, count, tally, 0)
    first = jnp.int32(0)
    for c in range(col_tiles):
        used[c] = 2 * first
        first = first + (sizes[c] + 1) // 2
    slots_ref[0] = first

    def place(b, carry):
        c = cols_ref[b]
        half = used[c]
        used[c] = half + 1
        slot_rows_ref[half] = rows_ref[b]
        slot_cols_ref[half // 2] = c
        tiles_ref[half] = values_ref[b].T
        return carry

    pull_values.wait()
    lax.fori_loop(0, count, place, 0)


def prepare(rows, cols, count, values, weight, col_tiles):
    blocks = values.shape[0]
    slot_total = -(-(blocks // 2 + col_tiles // 2) // SHORT) * SHORT
    smem = pl.BlockSpec(memory_space=pltpu.SMEM)
    vmem = pl.BlockSpec(memory_space=pltpu.VMEM)
    hbm = pl.BlockSpec(memory_space=pltpu.HBM)
    return pl.pallas_call(
        prepare_kernel,
        in_specs=[smem, smem, smem, hbm, hbm],
        out_specs=(vmem, smem, vmem),
        out_shape=(
            jax.ShapeDtypeStruct((2 * slot_total, BLK, BLK), bf16),
            jax.ShapeDtypeStruct((3 * slot_total + 1,), jnp.int32),
            jax.ShapeDtypeStruct(weight.shape, bf16),
        ),
        scratch_shapes=[
            pltpu.VMEM(values.shape, bf16),
            pltpu.VMEM(weight.shape, bf16),
            pltpu.SMEM((col_tiles,), jnp.int32),
            pltpu.SMEM((col_tiles,), jnp.int32),
            pltpu.SemaphoreType.DMA,
            pltpu.SemaphoreType.DMA,
        ],
        compiler_params=pltpu.CompilerParams(vmem_limit_bytes=VMEM_LIMIT),
    )(rows, cols, count, values, weight)


def hops_kernel(
    table_ref, dz, weight_hbm, tiles_hbm, out_hbm, dz_hbm,
    out, weight_t, tiles_ref, feats, first, second, weight_sem, tile_sems, out_sem, dz_sem,
):
    tiles = feats.shape[0]
    group = tiles // 2
    slot_total = tiles_ref.shape[0] // 2
    slot_rows_ref, slot_cols_ref, slots_ref = split_table(table_ref, slot_total)
    units = (slots_ref[0] + SHORT - 1) // SHORT
    trips = units // (LONG // SHORT)

    def pull_tiles(q):
        part = pl.ds(q * 2 * SHORT, 2 * SHORT)
        return pltpu.make_async_copy(tiles_hbm.at[part], tiles_ref.at[part], tile_sems.at[q])

    def push(c):
        part = pl.ds(pl.multiple_of(c * BLK, BLK), BLK)
        return pltpu.make_async_copy(out.at[part], out_hbm.at[part], out_sem)

    def start_tiles(q, carry):
        pull_tiles(q).start()
        return carry

    pull_weight = pltpu.make_async_copy(weight_hbm, weight_t, weight_sem)
    pull_weight.start()
    lax.fori_loop(0, units, start_tiles, 0)
    keep_dz = pltpu.make_async_copy(dz, dz_hbm, dz_sem)
    keep_dz.start()
    first[...] = jnp.zeros_like(first)
    second[...] = jnp.zeros_like(second)
    pull_weight.wait()
    for k in range(tiles // group):
        pushed = jnp.dot(
            dz[k * group * BLK : (k + 1) * group * BLK, :], weight_t[...], preferred_element_type=f32
        ).astype(bf16)
        for t in range(group):
            feats[k * group + t] = pushed[t * BLK : (t + 1) * BLK]

    def work(start, length, acc):
        for u in range(length):
            slot = start + u
            left = jnp.concatenate([tiles_ref[2 * slot], tiles_ref[2 * slot + 1]], axis=1)
            right = jnp.concatenate(
                [feats[slot_rows_ref[2 * slot]], feats[slot_rows_ref[2 * slot + 1]]], axis=0
            )
            c = slot_cols_ref[slot]
            acc[c] = acc[c] + jnp.dot(left, right, preferred_element_type=f32)

    def finish(c, carry):
        out[pl.ds(pl.multiple_of(c * BLK, BLK), BLK), :] = second[c].astype(bf16)
        push(c).start()
        return carry

    def first_hop(length, q, carry):
        for k in range(length // SHORT):
            pull_tiles(q * (length // SHORT) + k).wait()
        work(q * length, length, first)
        return carry

    def second_hop(length, q, done):
        work(q * length, length, second)
        after = (q + 1) * length
        upto = jnp.where(
            after < units * SHORT,
            slot_cols_ref[jnp.minimum(after, slot_total - 1)],
            tiles,
        )
        lax.fori_loop(done, upto, finish, 0)
        return upto

    rest = trips * (LONG // SHORT)
    lax.fori_loop(0, trips, functools.partial(first_hop, LONG), 0)
    lax.fori_loop(rest, units, functools.partial(first_hop, SHORT), 0)
    feats[...] = first[...].astype(bf16)
    done = lax.fori_loop(0, trips, functools.partial(second_hop, LONG), jnp.int32(0))
    lax.fori_loop(rest, units, functools.partial(second_hop, SHORT), done)
    keep_dz.wait()
    pltpu.make_async_copy(out, out_hbm, out_sem).wait()


def two_hops(table, dz, weight_t, tiles):
    verts, width = dz.shape
    col_tiles = verts // BLK
    smem = pl.BlockSpec(memory_space=pltpu.SMEM)
    hbm = pl.BlockSpec(memory_space=pltpu.HBM)
    return pl.pallas_call(
        hops_kernel,
        in_specs=[smem, pl.BlockSpec(memory_space=pltpu.VMEM), hbm, hbm],
        out_specs=(hbm, hbm),
        out_shape=(pltpu.HBM((verts, width), bf16),) * 2,
        scratch_shapes=[
            pltpu.VMEM((verts, width), bf16),
            pltpu.VMEM(weight_t.shape, bf16),
            pltpu.VMEM(tiles.shape, bf16),
            pltpu.VMEM((col_tiles, BLK, width), bf16),
            pltpu.VMEM((col_tiles, BLK, width), f32),
            pltpu.VMEM((col_tiles, BLK, width), f32),
            pltpu.SemaphoreType.DMA,
            pltpu.SemaphoreType.DMA((tiles.shape[0] // (2 * SHORT),)),
            pltpu.SemaphoreType.DMA,
            pltpu.SemaphoreType.DMA,
        ],
        compiler_params=pltpu.CompilerParams(vmem_limit_bytes=49 * 2**20),
    )(table, dz, weight_t, tiles)


def terms_kernel(left_hbm, right_hbm, out_ref, left, right, left_sem, right_sem):
    pull_left = pltpu.make_async_copy(left_hbm, left, left_sem)
    pull_right = pltpu.make_async_copy(right_hbm, right, right_sem)
    pull_left.start()
    pull_right.start()
    pull_left.wait()
    pull_right.wait()
    out_ref[...] = lax.dot_general(
        left[...], right[...], (((0,), (0,)), ((), ())), preferred_element_type=f32
    ).astype(bf16)


def gradient_terms(left, right):
    hbm = pl.BlockSpec(memory_space=pltpu.HBM)
    return pl.pallas_call(
        terms_kernel,
        in_specs=[hbm, hbm],
        out_specs=pl.BlockSpec(memory_space=pltpu.VMEM),
        out_shape=jax.ShapeDtypeStruct((left.shape[1], right.shape[1]), bf16),
        scratch_shapes=[
            pltpu.VMEM(left.shape, bf16),
            pltpu.VMEM(right.shape, bf16),
            pltpu.SemaphoreType.DMA,
            pltpu.SemaphoreType.DMA,
        ],
        compiler_params=pltpu.CompilerParams(vmem_limit_bytes=VMEM_LIMIT),
    )(left, right)


def exchange(field):
    return lax.all_to_all(field, "tm", split_axis=0, concat_axis=0, tiled=True)


def cluster_sum(terms, n):
    me = lax.axis_index("cluster")
    parts = terms.reshape(n, terms.shape[0] // n, terms.shape[1])

    def shift(array, k):
        return lax.ppermute(array, "cluster", [(i, (i + k) % n) for i in range(n)])

    def pick(stack, k):
        return lax.dynamic_index_in_dim(stack, k % n, 0, keepdims=False)

    total = pick(parts, me).astype(f32)
    for k in range(1, n):
        total = total + shift(pick(parts, me + k), k).astype(f32)
    share = total.astype(bf16)
    shares = jnp.stack([share] + [shift(share, k) for k in range(1, n)])
    whole = jnp.concatenate([pick(shares, me + n - q) for q in range(n)], axis=0)
    return whole.astype(f32)


def on_device(
    n_cluster, cotangent, propagated, weight, block_rows, block_cols, block_values, block_counts, band
):
    snaps, own, width = cotangent.shape
    verts = snaps * own
    dz = exchange(band_apply(band, cotangent, False)).reshape(verts, width)
    tiles, table, weight_t = prepare(
        block_rows[0, 0], block_cols[0, 0], block_counts[0], block_values[0, 0], weight[0], verts // BLK
    )
    second, dz = two_hops(table, dz, weight_t, tiles)
    input_grad = band_apply(band, exchange(second.reshape(snaps, own, width)), True)
    terms = gradient_terms(propagated[0], dz)
    weight_grad = cluster_sum(terms, n_cluster)
    return (input_grad, weight_grad[None])


def solution(mesh):
    placed = (
        P(None, ("cluster", "tm"), None),
        P("tm", "cluster", None),
        P("tm", None, None),
        P("tm", "cluster", None),
        P("tm", "cluster", None),
        P("tm", "cluster", None, None, None),
        P("tm", "cluster"),
        P(),
    )
    return jax.shard_map(
        functools.partial(on_device, mesh.shape["cluster"]),
        mesh=mesh,
        in_specs=placed,
        out_specs=(P(None, ("cluster", "tm"), None), P("tm", None, None)),
        check_vma=False,
    )
```
